256 devices in a mesh: band: 8 (over x, z_hi), grid: 32 (over z_lo, y, core).
Axes of the slice: x: 4, y: 4, z: 8 (z_hi: 2, z_lo: 4; z = z_hi * 4 + z_lo), core: 2. Of those that a mesh axis runs over, the one named last changes fastest.
Arguments:
- occupied: bfloat16 [128, 64, 64, 64], P(None, 'grid'), may hold values from -6 to 6
- empty: bfloat16 [128, 64, 64, 64], P(None, 'grid'), may hold values from -6 to 6
- pair_occ: int32 [512], P('band'), may hold values from 0 to 127
- pair_emp: int32 [512], P('band'), may hold values from 0 to 127
- g_cell: int32 [122880], P('grid'), may hold values from 0 to 8191, as said below
- eigvecs: bfloat16 [2, 122880, 2048], P(None, 'grid', 'band'), may hold values from -0.015625 to 0.015625
Outputs:
- projections: float32 [2, 512, 2048], P(None, 'grid', 'band')
The draws below stay inside these ranges and needn't reach their ends.
Inputs may be any that keep to these rules, and one draw needn't show every extreme that they name: `g_cell`: within each aligned block of 3840 entries the values are distinct, and 0 and 8191 are among them.
All inputs are finite; a program needn't handle non-finite values.
Results may differ from the reference program's by a relative error of at most 0.0029.
Values may be sent and summed in bfloat16 or wider, within the bound.
A program may use at most 128 MiB of HBM per device.

```python
import math
import jax
import jax.numpy as jnp
from jax import lax

NX = 64
NY = 64
NZ = 64
NG = 122880
NEIG = 2048
NOCC = 128
NEMP = 128
NPAIR_DEV = 64
NPAIRS = 512
NG_DEV = 3840
CELLS_DEV = 8192
N_GRID = 32


def draw_g_cell(key, part):
    key = jax.random.fold_in(key, 11)
    blocks = NG // NG_DEV
    subkeys = jax.random.split(key, blocks)

    def single(subkey):
        picking, ordering = jax.random.split(subkey)
        middle = jax.random.permutation(picking, CELLS_DEV - 2)[:NG_DEV - 2] + 1
        chosen = jnp.concatenate([jnp.array([0, CELLS_DEV - 1], jnp.int32), middle.astype(jnp.int32)])
        return jax.random.permutation(ordering, chosen)
    return jax.vmap(single)(subkeys).reshape(NG).astype(jnp.int32)


def plant(drawn, rng, smallest, largest):
    longest = drawn.shape.index(max(drawn.shape))
    spots = []
    for shift in (0, 1):
        where = [jax.random.randint(jax.random.fold_in(rng, axis), (), 0, length) for axis, length in enumerate(drawn.shape)]
        where[longest] = (where[longest] + shift) % drawn.shape[longest]
        spots.append(tuple(where))
    return drawn.at[spots[0]].set(smallest).at[spots[1]].set(largest)


def block_scale(own_key, shape, pieces, low, largest):
    factor_of, own = 1.0, jax.random.fold_in(own_key, 6)
    for axis_at, blocks in pieces:
        steps = jnp.exp(jax.random.uniform(jax.random.fold_in(own, axis_at), (blocks,), jnp.float32, low / len(pieces), largest / len(pieces)))
        factor_of = factor_of * jnp.repeat(steps, shape[axis_at] // blocks).reshape([-1 if axis == axis_at else 1 for axis in range(len(shape))])
    return factor_of


def normal_values(own_key, shape, width, most, pieces=(), held_as=jnp.bfloat16):
    entries = width * jax.random.normal(own_key, shape, jnp.float32)
    if pieces:
        entries = entries * block_scale(own_key, shape, pieces, -0.22, 0.18)
    return jnp.clip(entries, -most, most).astype(held_as)


def setup_inputs(seed: int = 0) -> dict:
    splits = jax.random.split(jax.random.key(seed), 7)
    return {
        "occupied": normal_values(splits[0], (NOCC, NX, NY, NZ), 1.0, 6.0, ((1, 32),)),
        "empty": normal_values(splits[1], (NEMP, NX, NY, NZ), 1.0, 6.0, ((1, 32),)),
        "pair_occ": plant(jax.random.randint(splits[2], (NPAIRS,), 0, NOCC), jax.random.fold_in(splits[2], 1), 0, NOCC - 1).astype(jnp.int32),
        "pair_emp": plant(jax.random.randint(splits[3], (NPAIRS,), 0, NEMP), jax.random.fold_in(splits[3], 1), 0, NEMP - 1).astype(jnp.int32),
        "g_cell": draw_g_cell(jax.random.fold_in(splits[6], 71), 0),
        "eigvecs": normal_values(splits[5], (2, NG, NEIG), NG ** -0.5, 0.015625, ((1, 32), (2, 8))),
    }


def reference(occupied, empty, pair_occ, pair_emp, g_cell, eigvecs):
    strip_cols = NY * NZ // N_GRID
    per_strip = NG // N_GRID
    owners = jnp.arange(NG, dtype=jnp.int32) // per_strip
    first_freq = g_cell // strip_cols
    column = owners * strip_cols + g_cell % strip_cols
    flat_index = (first_freq * (NY * NZ) + column).astype(jnp.int32)
    factor = 1.0 / math.sqrt(NX * NY * NZ)
    batches = NPAIRS // NPAIR_DEV

    def one_batch(indices):
        density = occupied[pair_occ[indices]].astype(jnp.float32) * empty[pair_emp[indices]].astype(jnp.float32)
        spectrum = jnp.fft.fftn(density, axes=(1, 2, 3)).reshape(indices.shape[0], NX * NY * NZ)
        chosen = spectrum[:, flat_index]
        real_part = (jnp.real(chosen) * factor).astype(jnp.bfloat16)
        imag_part = (jnp.imag(chosen) * factor).astype(jnp.bfloat16)
        return jnp.stack([real_part, imag_part])
    pair_ids = jnp.arange(NPAIRS, dtype=jnp.int32).reshape(batches, NPAIR_DEV)
    blocks = lax.map(one_batch, pair_ids)
    pair_g = jnp.transpose(blocks, (1, 0, 2, 3)).reshape(2, NPAIRS, NG)
    real_out = jnp.dot(pair_g[0], eigvecs[0], preferred_element_type=jnp.float32) + jnp.dot(pair_g[1], eigvecs[1], preferred_element_type=jnp.float32)
    imag_out = jnp.dot(pair_g[0], eigvecs[1], preferred_element_type=jnp.float32) - jnp.dot(pair_g[1], eigvecs[0], preferred_element_type=jnp.float32)
    return jnp.stack([real_out, imag_out])
```

```python
import functools
import math

import jax
import jax.numpy as jnp
import ml_dtypes
import numpy as np
from jax import lax
from jax.experimental import pallas as pl
from jax.experimental.pallas import tpu as pltpu
from jax.sharding import PartitionSpec as P

N = 64
LANES = 128
PAIRS = 64
STRIPS = 32
BANDS = 8
CELLS = 8192
G = 3840
EIG = 256
CHUNKS = 4
ROWS = G // CHUNKS
MESH = pl.DeviceIdType.MESH
F32 = jnp.float32
BF16 = jnp.bfloat16
VMEM_LIMIT = 56 * 1024 * 1024
HALF = math.sqrt(0.5)


def cadd(a, b):
    return (a[0] + b[0], a[1] + b[1])


def csub(a, b):
    return (a[0] - b[0], a[1] - b[1])


def turn(a, k, length):
    k = k % length
    if k == 0:
        return a
    if 4 * k == length:
        return (a[1], -a[0])
    if 2 * k == length:
        return (-a[0], -a[1])
    if 4 * k == 3 * length:
        return (-a[1], a[0])
    if 8 * k == length:
        return ((a[0] + a[1]) * HALF, (a[1] - a[0]) * HALF)
    if 8 * k == 3 * length:
        return ((a[1] - a[0]) * HALF, (a[0] + a[1]) * (-HALF))
    c, s = math.cos(2 * math.pi * k / length), math.sin(2 * math.pi * k / length)
    return (a[0] * c + a[1] * s, a[1] * c - a[0] * s)


def fft4(x):
    a, b, c, d = cadd(x[0], x[2]), csub(x[0], x[2]), cadd(x[1], x[3]), csub(x[1], x[3])
    return [cadd(a, c), (b[0] + d[1], b[1] - d[0]), csub(a, c), (b[0] - d[1], b[1] + d[0])]


def fft8(x):
    even, odd = fft4(x[0::2]), fft4(x[1::2])
    odd = [turn(odd[k], k, 8) for k in range(4)]
    return [cadd(even[k], odd[k]) for k in range(4)] + [csub(even[k], odd[k]) for k in range(4)]


def rfft8(x):
    def four(v):
        a, b, c, d = v[0] + v[2], v[0] - v[2], v[1] + v[3], v[1] - v[3]
        return a + c, (b, -d), a - c

    e0, e1, e2 = four(x[0::2])
    o0, o1, o2 = four(x[1::2])
    o1 = turn(o1, 1, 8)
    low = csub(e1, o1)
    return [e0 + o0, cadd(e1, o1), (e2, -o2), (low[0], -low[1]), e0 - o0]


def z_tables():
    index = np.arange(N)
    angle = (index[:, None] * index[None, :] % N) * (2 * np.pi / N)
    c, s = np.cos(angle) / 512.0, np.sin(angle) / 512.0
    table = np.block([[c, s], [-s, c], [c, -s], [-s, -c]]).astype(np.float32)
    high = table.astype(ml_dtypes.bfloat16)
    low = (table - high.astype(np.float32)).astype(ml_dtypes.bfloat16)
    return np.concatenate([high, high], axis=1), low


def split(value):
    high = value.astype(BF16)
    return high, (value - high.astype(F32)).astype(BF16)


def dot(a, b):
    return jnp.dot(a, b, preferred_element_type=F32)


def one_hot(pairs_ref):
    row = pairs_ref[...]
    row = jnp.concatenate([row, row], axis=1)
    r = lax.broadcasted_iota(jnp.int32, (2 * LANES, LANES), 0)
    lane = lax.broadcasted_iota(jnp.int32, (2 * LANES, LANES), 1)
    hit = (r % LANES == row) & (r // LANES == lane // PAIRS)
    return jnp.where(hit, 1.0, 0.0).astype(BF16)


def density(occ_ref, emp_ref, pocc_ref, pemp_ref, dens):
    pick_occ, pick_emp = one_hot(pocc_ref), one_hot(pemp_ref)
    rows = 512

    @pl.loop(0, N * N // rows)
    def _(step):
        at = pl.ds(pl.multiple_of(step * rows, rows), rows)
        occ = jnp.concatenate([occ_ref[0, at, :], occ_ref[1, at, :]], axis=1)
        emp = jnp.concatenate([emp_ref[0, at, :], emp_ref[1, at, :]], axis=1)
        dens[at, :] = dot(occ, pick_occ) * dot(emp, pick_emp)


def transform_y(dens, spec, work):
    @pl.loop(0, 8)
    def _(tile):
        at = pl.multiple_of(tile * 8, 8)
        for n2 in range(8):
            outs = rfft8([dens[pl.ds((8 * n1 + n2) * N + at, 8), :] for n1 in range(8)])
            work[0, n2, 0] = outs[0]
            for k1 in (1, 2, 3):
                re, im = turn(outs[k1], n2 * k1, 64)
                work[k1, n2, 0] = re
                work[k1, n2, 1] = im
            angle = 2 * math.pi * n2 * 4 / 64
            work[4, n2, 0] = outs[4] * math.cos(angle)
            work[4, n2, 1] = outs[4] * (-math.sin(angle))
        outs = rfft8([work[0, n2, 0] for n2 in range(8)])
        zero = jnp.zeros_like(outs[0])
        for k2 in range(5):
            re, im = (outs[k2], zero) if k2 in (0, 4) else outs[k2]
            spec[8 * k2, pl.ds(at, 8), :] = re
            spec[8 * k2, pl.ds(N + at, 8), :] = im
        for k1 in (1, 2, 3, 4):
            outs = fft8([(work[k1, n2, 0], work[k1, n2, 1]) for n2 in range(8)])
            for k2 in range(8 if k1 < 4 else 4):
                ky = k1 + 8 * k2
                re, im = outs[k2]
                if ky > 32:
                    ky, im = 64 - ky, -im
                spec[ky, pl.ds(at, 8), :] = re
                spec[ky, pl.ds(N + at, 8), :] = im


def planes_kernel(
    pocc_ref, pemp_ref, occ_ref, emp_ref, t1_ref, t2_ref, recv,
    dens, spec, work, send, send_sems, recv_sems, local_sem,
):
    band = lax.axis_index("band")
    me = lax.axis_index("grid")
    barrier = pltpu.get_barrier_semaphore()

    @pl.loop(1, STRIPS)
    def _(k):
        pl.semaphore_signal(barrier, inc=1, device_id=(band, (me + k) % STRIPS), device_id_type=MESH)

    density(occ_ref, emp_ref, pocc_ref, pemp_ref, dens)
    transform_y(dens, spec, work)
    pl.semaphore_wait(barrier, STRIPS - 1)

    def copy(strip):
        return pltpu.make_async_remote_copy(
            src_ref=send.at[strip], dst_ref=recv.at[me], send_sem=send_sems.at[strip],
            recv_sem=recv_sems.at[me], device_id=(band, strip), device_id_type=MESH,
        )

    def start(strip):
        @pl.when(strip != me)
        def _():
            copy(strip).start()

    @pl.loop(0, 16)
    def _(step):
        j = (me + step) % 16
        h0, l0 = split(spec[2 * j])
        h1, l1 = split(spec[2 * j + 1])
        high = jnp.concatenate([h0, h1], axis=1)
        low = jnp.concatenate([l0, l1], axis=1)
        out = dot(t1_ref[...], jnp.concatenate([high, low], axis=0)) + dot(t2_ref[...], high)
        out = out.astype(BF16)
        send[j, 0] = out[:LANES, :LANES]
        send[j, 1] = out[:LANES, LANES:]
        start(j)

        @pl.when(j > 0)
        def _():
            send[32 - j, 0] = out[LANES:, :LANES]

        send[31 - j, 1] = out[LANES:, LANES:]

    h0, l0 = split(spec[32])
    out = dot(t1_ref[:LANES, :], jnp.concatenate([h0, l0], axis=0)) + dot(t2_ref[:LANES, :], h0)
    send[16, 0] = out.astype(BF16)

    @pl.loop(0, 16)
    def _(step):
        start(16 + (me + step) % 16)

    own = pltpu.make_async_copy(send.at[me], recv.at[me], local_sem)
    own.start()
    own.wait()

    @pl.loop(1, STRIPS)
    def _(k):
        other = (me + k) % STRIPS
        copy(other).wait_send()
        pltpu.make_async_remote_copy(
            src_ref=send.at[other], dst_ref=recv.at[other], send_sem=send_sems.at[other],
            recv_sem=recv_sems.at[other], device_id=(band, other), device_id_type=MESH,
        ).wait_recv()


def planes(pocc, pemp, occ, emp):
    t1, t2 = z_tables()
    vmem = pl.BlockSpec(memory_space=pltpu.VMEM)
    return pl.pallas_call(
        planes_kernel,
        out_shape=jax.ShapeDtypeStruct((STRIPS, 2, 2 * N, LANES), BF16),
        in_specs=[vmem] * 6,
        out_specs=pl.BlockSpec(memory_space=pl.ANY),
        scratch_shapes=[
            pltpu.VMEM((N * N, LANES), F32),
            pltpu.VMEM((33, 2 * N, LANES), F32),
            pltpu.VMEM((5, 8, 2, 8, LANES), F32),
            pltpu.VMEM((STRIPS, 2, 2 * N, LANES), BF16),
            pltpu.SemaphoreType.DMA((STRIPS,)),
            pltpu.SemaphoreType.DMA((STRIPS,)),
            pltpu.SemaphoreType.DMA,
        ],
        compiler_params=pltpu.CompilerParams(
            collective_id=0, has_side_effects=True, vmem_limit_bytes=VMEM_LIMIT
        ),
        name="planes",
    )(pocc, pemp, occ, emp, jnp.asarray(t1), jnp.asarray(t2))


def transform_x(recv, cells, work):
    lane = lax.broadcasted_iota(jnp.int32, (8, LANES), 1)
    left = lane < PAIRS

    @pl.loop(0, 2 * 4)
    def _(tile):
        kyl = tile // 4
        at = pl.multiple_of((tile % 4) * 16, 16)
        for n2 in range(8):
            outs = fft4(
                [
                    (
                        recv[8 * n1 + n2, kyl, pl.ds(at, 16), :].astype(F32),
                        recv[8 * n1 + n2, kyl, pl.ds(N + at, 16), :].astype(F32),
                    )
                    for n1 in range(4)
                ]
            )
            for k1 in range(4):
                re, im = turn(outs[k1], n2 * k1, 32)
                work[k1, n2, 0] = re
                work[k1, n2, 1] = im
        for half in range(2):
            rows = slice(8 * half, 8 * half + 8)
            for k1 in range(4):
                outs = fft8([(work[k1, n2, 0, rows], work[k1, n2, 1, rows]) for n2 in range(8)])
                for k2 in range(8):
                    kx = k1 + 4 * k2
                    re, im = outs[k2]
                    c = jnp.where(left, 1.0, math.cos(2 * math.pi * kx / 64))
                    s = jnp.where(left, 0.0, math.sin(2 * math.pi * kx / 64))
                    re, im = re * c + im * s, im * c - re * s
                    even = jnp.where(left, re, pltpu.roll(im, PAIRS, axis=1))
                    odd = jnp.where(left, pltpu.roll(re, PAIRS, axis=1), im)
                    cell = kyl * N + at + 8 * half
                    cells[pl.ds(kx * LANES + cell, 8), :] = even + odd
                    cells[pl.ds((kx + 32) * LANES + cell, 8), :] = even - odd


def pick(cell_ref, cells, rows, out):
    block = 16

    @pl.loop(0, G // block)
    def _(step):
        at = pl.multiple_of(step * block, block)
        for i in range(block):
            rows[pl.ds(at + i, 1), :] = cells[pl.ds(cell_ref[at + i], 1), :]

    @pl.loop(0, G // 128)
    def _(step):
        at = pl.ds(pl.multiple_of(step * 128, 128), 128)
        out[at, :] = rows[at, :].astype(BF16)


def columns_kernel(cell_ref, recv, out, cells, work, rows):
    transform_x(recv, cells, work)
    pick(cell_ref, cells, rows, out)


def columns(g_cell, recv):
    vmem = pl.BlockSpec(memory_space=pltpu.VMEM)
    return pl.pallas_call(
        columns_kernel,
        out_shape=jax.ShapeDtypeStruct((G, LANES), BF16),
        in_specs=[pl.BlockSpec(memory_space=pltpu.SMEM), vmem],
        out_specs=vmem,
        scratch_shapes=[
            pltpu.VMEM((CELLS, LANES), F32),
            pltpu.VMEM((4, 8, 2, 16, LANES), F32),
            pltpu.VMEM((G, LANES), F32),
        ],
        compiler_params=pltpu.CompilerParams(vmem_limit_bytes=VMEM_LIMIT),
        name="columns",
    )(g_cell, recv)


def project_kernel(
    spectra, eig, out, held, sums, parts, z_send, z_recv, x_send, x_recv, f_send, f_recv, r_send, r_recv,
):
    band = lax.axis_index("band")
    me = lax.axis_index("grid")
    right, left, opposite = (band + 2) % BANDS, (band + 6) % BANDS, (band + 4) % BANDS

    def other(b):
        return b + 1 - 2 * (b % 2)

    partner = other(band)
    barrier = pltpu.get_barrier_semaphore()
    for b in (right, left, partner):
        pl.semaphore_signal(barrier, inc=1, device_id=(b, me), device_id_type=MESH)

    @pl.loop(1, STRIPS)
    def _(k):
        pl.semaphore_signal(barrier, inc=1, device_id=(band, (me + k) % STRIPS), device_id_type=MESH)

    pl.semaphore_wait(barrier, STRIPS + 2)

    def at(c):
        return pl.ds(c * ROWS, ROWS)

    def move(src, block, c, send_sem, recv_sem, to):
        return pltpu.make_async_remote_copy(
            src_ref=src, dst_ref=held.at[block, at(c)], send_sem=send_sem, recv_sem=recv_sem,
            device_id=(to, me), device_id_type=MESH,
        )

    def z_copy(c):
        return move(spectra.at[at(c)], band, c, z_send.at[c], z_recv.at[c], partner)

    def x_copy(kind, side, c):
        src = spectra.at[at(c)] if kind == 0 else held.at[partner, at(c)]
        return move(
            src, partner if kind else band, c, x_send.at[kind, side, c], x_recv.at[kind, side, c],
            left if side else right,
        )

    def f_copy(kind, c):
        side = 0 if c < CHUNKS // 2 else 1
        block = right if side else left
        if kind:
            block = other(block)
        return move(
            held.at[block, at(c)], block, c, f_send.at[kind, c], f_recv.at[kind, c],
            left if side else right,
        )

    def multiply(src, block):
        def body(c, acc):
            rows = pl.ds(pl.multiple_of(c * 480, 480), 480)
            s = src[rows, :]
            dims = (((0,), (0,)), ((), ()))
            return (
                acc[0] + lax.dot_general(s, eig[0, rows, :], dims, preferred_element_type=F32),
                acc[1] + lax.dot_general(s, eig[1, rows, :], dims, preferred_element_type=F32),
            )

        zero = jnp.zeros((2 * PAIRS, EIG), F32)
        p0, p1 = lax.fori_loop(0, G // 480, body, (zero, zero))
        sums[block, :, :EIG] = p0[:PAIRS] + p1[PAIRS:]
        sums[block, :, EIG:] = p1[:PAIRS] - p0[PAIRS:]
        for i in range(4):
            strip = block * 4 + i

            @pl.when(strip != me)
            def _():
                r_copy(strip).start()

    def r_copy(strip):
        rows = pl.ds(pl.multiple_of((strip % 4) * 16, 16), 16)
        return pltpu.make_async_remote_copy(
            src_ref=sums.at[strip // 4, rows], dst_ref=parts.at[me], send_sem=r_send.at[strip],
            recv_sem=r_recv.at[me], device_id=(band, strip), device_id_type=MESH,
        )

    for c in range(CHUNKS):
        z_copy(c).start()
        x_copy(0, 0, c).start()
        x_copy(0, 1, c).start()

    def arrive(kind, c):
        x_copy(kind, 0, c).wait_recv()
        x_copy(kind, 1, c).wait_recv()
        f_copy(kind, c).start()

    multiply(spectra, band)
    for c in range(CHUNKS):
        arrive(0, c)
        z_copy(c).wait_recv()
        x_copy(1, 0, c).start()
        x_copy(1, 1, c).start()
    multiply(held.at[left], left)
    multiply(held.at[right], right)
    multiply(held.at[partner], partner)
    for c in range(CHUNKS):
        f_copy(0, c).wait_recv()
        arrive(1, c)
    multiply(held.at[opposite], opposite)
    multiply(held.at[other(left)], other(left))
    multiply(held.at[other(right)], other(right))
    for c in range(CHUNKS):
        f_copy(1, c).wait_recv()
    multiply(held.at[other(opposite)], other(opposite))

    own = pl.ds(pl.multiple_of((me % 4) * 16, 16), 16)

    def add(k, total):
        src = (me + k) % STRIPS
        pltpu.make_async_remote_copy(
            src_ref=parts.at[src], dst_ref=parts.at[src], send_sem=r_send.at[src],
            recv_sem=r_recv.at[src], device_id=(band, src), device_id_type=MESH,
        ).wait_recv()
        return total + parts[src]

    total = lax.fori_loop(1, STRIPS, add, sums[me // 4, own, :])
    out[0] = total[:, :EIG]
    out[1] = total[:, EIG:]

    for c in range(CHUNKS):
        z_copy(c).wait_send()
        for kind in range(2):
            f_copy(kind, c).wait_send()
            for side in range(2):
                x_copy(kind, side, c).wait_send()

    @pl.loop(1, STRIPS)
    def _(k):
        r_copy((me + k) % STRIPS).wait_send()


def project(spectra, eigvecs):
    vmem = pl.BlockSpec(memory_space=pltpu.VMEM)
    return pl.pallas_call(
        project_kernel,
        out_shape=jax.ShapeDtypeStruct((2, 16, EIG), F32),
        in_specs=[vmem, vmem],
        out_specs=vmem,
        scratch_shapes=[
            pltpu.VMEM((BANDS, G, LANES), BF16),
            pltpu.VMEM((BANDS, PAIRS, 2 * EIG), F32),
            pltpu.VMEM((STRIPS, 16, 2 * EIG), F32),
            pltpu.SemaphoreType.DMA((CHUNKS,)),
            pltpu.SemaphoreType.DMA((CHUNKS,)),
            pltpu.SemaphoreType.DMA((2, 2, CHUNKS)),
            pltpu.SemaphoreType.DMA((2, 2, CHUNKS)),
            pltpu.SemaphoreType.DMA((2, CHUNKS)),
            pltpu.SemaphoreType.DMA((2, CHUNKS)),
            pltpu.SemaphoreType.DMA((STRIPS,)),
            pltpu.SemaphoreType.DMA((STRIPS,)),
        ],
        compiler_params=pltpu.CompilerParams(
            collective_id=1, has_side_effects=True, vmem_limit_bytes=VMEM_LIMIT
        ),
        name="project",
    )(spectra, eigvecs)


def shards(occupied, empty, pair_occ, pair_emp, g_cell, eigvecs):
    occ = jnp.transpose(occupied, (1, 2, 3, 0)).reshape(2, N * N, LANES)
    emp = jnp.transpose(empty, (1, 2, 3, 0)).reshape(2, N * N, LANES)
    recv = planes(pair_occ.reshape(1, PAIRS), pair_emp.reshape(1, PAIRS), occ, emp)
    spectra = columns(g_cell, recv)
    return project(spectra, eigvecs)


def solution(mesh):
    in_specs = (
        P(None, "grid", None, None),
        P(None, "grid", None, None),
        P("band"),
        P("band"),
        P("grid"),
        P(None, "grid", "band"),
    )
    out_specs = P(None, "grid", "band")
    return jax.shard_map(shards, mesh=mesh, in_specs=in_specs, out_specs=out_specs, check_vma=False)
```

```python
import math

import jax
import jax.numpy as jnp
import ml_dtypes
import numpy as np
from jax import lax
from jax.experimental import pallas as pl
from jax.experimental.pallas import tpu as pltpu
from jax.sharding import PartitionSpec as P

N = 64
LANES = 128
PAIRS = 64
STRIPS = 32
BANDS = 8
CELLS = 8192
G = 3840
EIG = 256
ROWS = G // 2
XS = 4
SETS = 2
MESH = pl.DeviceIdType.MESH
F32 = jnp.float32
BF16 = jnp.bfloat16
VMEM_LIMIT = 56 * 1024 * 1024
HALF = math.sqrt(0.5)


def cadd(a, b):
    return (a[0] + b[0], a[1] + b[1])


def csub(a, b):
    return (a[0] - b[0], a[1] - b[1])


def turn(a, k, length):
    k = k % length
    if k == 0:
        return a
    if 4 * k == length:
        return (a[1], -a[0])
    if 2 * k == length:
        return (-a[0], -a[1])
    if 4 * k == 3 * length:
        return (-a[1], a[0])
    if 8 * k == length:
        return ((a[0] + a[1]) * HALF, (a[1] - a[0]) * HALF)
    if 8 * k == 3 * length:
        return ((a[1] - a[0]) * HALF, (a[0] + a[1]) * (-HALF))
    c, s = math.cos(2 * math.pi * k / length), math.sin(2 * math.pi * k / length)
    return (a[0] * c + a[1] * s, a[1] * c - a[0] * s)


def fft4(x):
    a, b, c, d = cadd(x[0], x[2]), csub(x[0], x[2]), cadd(x[1], x[3]), csub(x[1], x[3])
    return [cadd(a, c), (b[0] + d[1], b[1] - d[0]), csub(a, c), (b[0] - d[1], b[1] + d[0])]


def fft8(x):
    even, odd = fft4(x[0::2]), fft4(x[1::2])
    odd = [turn(odd[k], k, 8) for k in range(4)]
    return [cadd(even[k], odd[k]) for k in range(4)] + [csub(even[k], odd[k]) for k in range(4)]


def rfft8(x):
    def four(v):
        a, b, c, d = v[0] + v[2], v[0] - v[2], v[1] + v[3], v[1] - v[3]
        return a + c, (b, -d), a - c

    e0, e1, e2 = four(x[0::2])
    o0, o1, o2 = four(x[1::2])
    o1 = turn(o1, 1, 8)
    low = csub(e1, o1)
    return [e0 + o0, cadd(e1, o1), (e2, -o2), (low[0], -low[1]), e0 - o0]


def z_tables():
    index = np.arange(N)
    angle = (index[:, None] * index[None, :] % N) * (2 * np.pi / N)
    c, s = np.cos(angle) / 512.0, np.sin(angle) / 512.0
    table = np.block([[c, s], [-s, c], [c, -s], [-s, -c]]).astype(np.float32)
    high = table.astype(ml_dtypes.bfloat16)
    low = (table - high.astype(np.float32)).astype(ml_dtypes.bfloat16)
    return np.concatenate([high, high], axis=1), low


def split(value):
    high = value.astype(BF16)
    return high, (value - high.astype(F32)).astype(BF16)


def dot(a, b):
    return jnp.dot(a, b, preferred_element_type=F32)


def one_hot(row):
    r = lax.broadcasted_iota(jnp.int32, (2 * LANES, LANES), 0)
    lane = lax.broadcasted_iota(jnp.int32, (2 * LANES, LANES), 1)
    hit = (r % LANES == row) & (r // LANES == lane // PAIRS)
    return jnp.where(hit, 1.0, 0.0).astype(BF16)


def density(occ_ref, emp_ref, pairs, dens):
    pick_occ, pick_emp = one_hot(pairs[0:1, :]), one_hot(pairs[1:2, :])
    rows = 512

    @pl.loop(0, N * N // rows)
    def _(step):
        at = pl.ds(pl.multiple_of(step * rows, rows), rows)
        occ = jnp.concatenate([occ_ref[0, at, :], occ_ref[1, at, :]], axis=1)
        emp = jnp.concatenate([emp_ref[0, at, :], emp_ref[1, at, :]], axis=1)
        dens[at, :] = dot(occ, pick_occ) * dot(emp, pick_emp)


def transform_y(dens, spec, work):
    @pl.loop(0, 8)
    def _(tile):
        at = pl.multiple_of(tile * 8, 8)
        for n2 in range(8):
            outs = rfft8([dens[pl.ds((8 * n1 + n2) * N + at, 8), :] for n1 in range(8)])
            work[0, n2, 0] = outs[0]
            for k1 in (1, 2, 3):
                re, im = turn(outs[k1], n2 * k1, 64)
                work[k1, n2, 0] = re
                work[k1, n2, 1] = im
            angle = 2 * math.pi * n2 * 4 / 64
            work[4, n2, 0] = outs[4] * math.cos(angle)
            work[4, n2, 1] = outs[4] * (-math.sin(angle))
        outs = rfft8([work[0, n2, 0] for n2 in range(8)])
        zero = jnp.zeros_like(outs[0])
        for k2 in range(5):
            re, im = (outs[k2], zero) if k2 in (0, 4) else outs[k2]
            spec[8 * k2, pl.ds(at, 8), :] = re
            spec[8 * k2, pl.ds(N + at, 8), :] = im
        for k1 in (1, 2, 3, 4):
            outs = fft8([(work[k1, n2, 0], work[k1, n2, 1]) for n2 in range(8)])
            for k2 in range(8 if k1 < 4 else 4):
                ky = k1 + 8 * k2
                re, im = outs[k2]
                if ky > 32:
                    ky, im = 64 - ky, -im
                spec[ky, pl.ds(at, 8), :] = re
                spec[ky, pl.ds(N + at, 8), :] = im


def transform_x(recv, cells, work):
    lane = lax.broadcasted_iota(jnp.int32, (8, LANES), 1)
    left = lane < PAIRS

    @pl.loop(0, 2 * 4)
    def _(tile):
        kyl = tile // 4
        at = pl.multiple_of((tile % 4) * 16, 16)
        for n2 in range(8):
            outs = fft4(
                [
                    (
                        recv[8 * n1 + n2, kyl, pl.ds(at, 16), :].astype(F32),
                        recv[8 * n1 + n2, kyl, pl.ds(N + at, 16), :].astype(F32),
                    )
                    for n1 in range(4)
                ]
            )
            for k1 in range(4):
                re, im = turn(outs[k1], n2 * k1, 32)
                work[k1, n2, 0] = re
                work[k1, n2, 1] = im
        for half in range(2):
            rows = slice(8 * half, 8 * half + 8)
            for k1 in range(4):
                outs = fft8([(work[k1, n2, 0, rows], work[k1, n2, 1, rows]) for n2 in range(8)])
                for k2 in range(8):
                    kx = k1 + 4 * k2
                    re, im = outs[k2]
                    c = jnp.where(left, 1.0, math.cos(2 * math.pi * kx / 64))
                    s = jnp.where(left, 0.0, math.sin(2 * math.pi * kx / 64))
                    re, im = re * c + im * s, im * c - re * s
                    even = jnp.where(left, re, pltpu.roll(im, PAIRS, axis=1))
                    odd = jnp.where(left, pltpu.roll(re, PAIRS, axis=1), im)
                    cell = kyl * N + at + 8 * half
                    cells[pl.ds(kx * LANES + cell, 8), :] = even + odd
                    cells[pl.ds((kx + 32) * LANES + cell, 8), :] = even - odd


def pick(cell_ref, cells, rows, out):
    block = 16

    @pl.loop(0, G // block)
    def _(step):
        at = pl.multiple_of(step * block, block)
        for i in range(block):
            rows[pl.ds(at + i, 1), :] = cells[pl.ds(cell_ref[at + i], 1), :]

    @pl.loop(0, G // 128)
    def _(step):
        at = pl.ds(pl.multiple_of(step * 128, 128), 128)
        out[at, :] = rows[at, :].astype(BF16)


def kernel(
    cell_ref, pairs_ref, occ_ref, emp_ref, t1_ref, t2_ref, eig_ref, out,
    lists, dens, spec, work_y, send, recv, cells, work_x, rows, own, held, eigs, sums, parts, done, final,
    list_sems, a_send, a_recv, local_sems, e_send, e_recv, x_send, x_recv, r_send, r_recv, f_send, f_recv,
):
    band = lax.axis_index("band")
    me = lax.axis_index("grid")
    x, zh = band // 2, band % 2
    zl, low = me // 8, me % 8
    core = me % 2
    z = zh * 4 + zl
    half = x % 2

    def peer(strip):
        steps = (strip // 8 - zl + 4) % 4
        side = (zl // 2 + core + strip) % 2
        away = steps - 4 * (steps // 3) - 4 * side * (steps // 2 - steps // 3)
        return (2 * x + ((z + away + 8) % 8) // 4, strip)

    def along_x(step):
        return (2 * ((x + step) % XS) + zh, me)

    partner_z = (band + 1 - 2 * zh, me)
    partner_x = (band + 2 - 4 * half, me)

    barrier = pltpu.get_barrier_semaphore()

    def greet(device):
        pl.semaphore_signal(barrier, inc=1, device_id=device, device_id_type=MESH)

    def remote(src, dst, send_sem, recv_sem, device):
        return pltpu.make_async_remote_copy(
            src_ref=src, dst_ref=dst, send_sem=send_sem, recv_sem=recv_sem, device_id=device, device_id_type=MESH
        )

    @pl.loop(1, STRIPS)
    def _(k):
        greet(peer((me + k) % STRIPS))

    greet(partner_z)
    for step in (1, 2, 3):
        greet(along_x(step))

    @pl.loop(0, 16)
    def _(k):
        source = (k // 4) * 8 + 2 * (low % 4) + k % 2
        to = 2 * (2 * (x // 2) + (k // 2) % 2) + zh

        @pl.when(jnp.logical_or(source != me, to != band))
        def _():
            greet((to, source))

    mine = jnp.where(jnp.logical_or(low == 0, low == 7), 1, 0)
    list_own = pltpu.make_async_copy(pairs_ref, lists.at[zh], local_sems.at[0])
    list_own.start()
    eig_own = [
        pltpu.make_async_copy(
            eig_ref.at[i, pl.ds(pl.multiple_of(half * ROWS, ROWS), ROWS)],
            eigs.at[:, pl.ds(pl.multiple_of(half * 2 * EIG + i * EIG, EIG), EIG)],
            local_sems.at[1 + i],
        )
        for i in range(2)
    ]
    for copy in eig_own:
        copy.start()
    list_own.wait()
    pl.semaphore_wait(barrier, 31 + 1 + 3 + 16 - mine)

    list_copy = remote(lists.at[zh], lists.at[zh], list_sems.at[0], list_sems.at[1], partner_z)
    list_copy.start()
    eig_copy = [
        remote(
            eig_ref.at[i, pl.ds(pl.multiple_of((1 - half) * ROWS, ROWS), ROWS)],
            eigs.at[:, pl.ds(pl.multiple_of(half * 2 * EIG + i * EIG, EIG), EIG)],
            e_send.at[i], e_recv.at[i], partner_x,
        )
        for i in range(2)
    ]
    for copy in eig_copy:
        copy.start()
    list_copy.wait()

    def a_copy(which, strip):
        return remote(
            send.at[which, strip], recv.at[which, me], a_send.at[which, strip], a_recv.at[which, me], peer(strip)
        )

    def planes(which):
        density(occ_ref, emp_ref, lists[which], dens)
        transform_y(dens, spec, work_y)

        def start(strip):
            @pl.when(strip != me)
            def _():
                if which:
                    a_copy(0, strip).wait_send()
                a_copy(which, strip).start()

        @pl.loop(0, 16)
        def _(step):
            j = (me + step) % 16
            h0, l0 = split(spec[2 * j])
            h1, l1 = split(spec[2 * j + 1])
            high = jnp.concatenate([h0, h1], axis=1)
            low_part = jnp.concatenate([l0, l1], axis=1)
            both = dot(t1_ref[...], jnp.concatenate([high, low_part], axis=0)) + dot(t2_ref[...], high)
            both = both.astype(BF16)
            send[which, j, 0] = both[:LANES, :LANES]
            send[which, j, 1] = both[:LANES, LANES:]
            start(j)

            @pl.when(j > 0)
            def _():
                send[which, 32 - j, 0] = both[LANES:, :LANES]

            send[which, 31 - j, 1] = both[LANES:, LANES:]

        h0, l0 = split(spec[32])
        one = dot(t1_ref[:LANES, :], jnp.concatenate([h0, l0], axis=0)) + dot(t2_ref[:LANES, :], h0)
        send[which, 16, 0] = one.astype(BF16)

        @pl.loop(0, 16)
        def _(step):
            start(16 + (me + step) % 16)

        copy = pltpu.make_async_copy(send.at[which, me], recv.at[which, me], local_sems.at[3])
        copy.start()
        copy.wait()

    def x_copy(which, step):
        part = half if step == 2 else 1 - half
        return remote(
            own.at[which, pl.ds(pl.multiple_of(part * ROWS, ROWS), ROWS)], held.at[which, x],
            x_send.at[which, step - 1], x_recv.at[which, step - 1], along_x(step),
        )

    def columns(which):
        @pl.loop(1, STRIPS)
        def _(k):
            source = (me + k) % STRIPS
            remote(
                send.at[which, source], recv.at[which, source], a_send.at[which, source],
                a_recv.at[which, source], peer(source),
            ).wait_recv()

        transform_x(recv.at[which], cells, work_x)
        pick(cell_ref, cells, rows, own.at[which])
        for step in (1, 3, 2):
            x_copy(which, step).start()

    def r_copy(block, to):
        return remote(
            sums.at[block, pl.ds(pl.multiple_of(to * 8, 8), 8)], parts.at[low, block],
            r_send.at[block, to], r_recv.at[low, block], (band, zl * 8 + to),
        )

    def multiply(src, block):
        @pl.loop(0, 2)
        def _(q):
            at = pl.multiple_of(q * 2 * EIG, 2 * EIG)
            part = lax.dot_general(
                src[...], eigs[:, pl.ds(at, 2 * EIG)], (((0,), (0,)), ((), ())), preferred_element_type=F32
            )
            sums[block, :, pl.ds(at, EIG)] = part[:PAIRS, :EIG] + part[PAIRS:, EIG:]
            sums[block, :, pl.ds(at + EIG, EIG)] = part[:PAIRS, EIG:] - part[PAIRS:, :EIG]

        @pl.loop(1, 8)
        def _(k):
            r_copy(block, (low + k) % 8).start()

    def multiply_own(which):
        at = pl.ds(pl.multiple_of(half * ROWS, ROWS), ROWS)
        multiply(own.at[which, at], 2 * x + which)

    def multiply_from(which, step):
        x_copy(which, step).wait_recv()
        source = (x - step + XS) % XS
        multiply(held.at[which, source], 2 * source + which)

    def f_copy(block, q):
        owner = (block // 2) * 8 + 4 * (block % 2) + low // 2
        slot = (zl * 2 + half) * 2 + low % 2
        return remote(
            done.at[block, :, pl.ds(q * 2 * EIG, 2 * EIG)], final.at[slot],
            f_send.at[block, q], f_recv.at[slot], (2 * (2 * (x // 2) + q) + zh, owner),
        )

    def here(block, q):
        owner = (block // 2) * 8 + 4 * (block % 2) + low // 2
        return jnp.logical_and(owner == me, half == q)

    def reduce(which):
        @pl.loop(0, XS)
        def _(step):
            block = 2 * ((x + XS - step) % XS) + which
            mine_at = pl.ds(pl.multiple_of(low * 8, 8), 8)

            def add(k, total):
                source = (low + k) % 8
                remote(
                    sums.at[block, mine_at], parts.at[source, block], r_send.at[block, source],
                    r_recv.at[source, block], (band, zl * 8 + source),
                ).wait_recv()
                return total + parts[source, block]

            done[block] = lax.fori_loop(1, 8, add, sums[block, mine_at, :])
            for q in range(2):
                local = here(block, q)

                @pl.when(jnp.logical_not(local))
                def _():
                    f_copy(block, q).start()

                @pl.when(local)
                def _():
                    slot = (zl * 2 + half) * 2 + low % 2
                    final[slot] = done[block, :, q * 2 * EIG : (q + 1) * 2 * EIG]

    planes(0)
    planes(1)
    columns(0)
    for copy in eig_own:
        copy.wait()
    for copy in eig_copy:
        copy.wait_recv()
    multiply_own(0)
    columns(1)
    multiply_own(1)
    for step in (1, 3, 2):
        multiply_from(0, step)
    multiply_from(1, 1)
    multiply_from(1, 3)
    reduce(0)
    multiply_from(1, 2)
    reduce(1)

    for row in range(2):
        total = jnp.zeros((8, 2 * EIG), F32)
        for k in range(8):
            slot = 2 * k + row
            local = jnp.logical_and(
                jnp.logical_and(zl * 2 + half == k, low % 2 == row), jnp.logical_or(low == 0, low == 7)
            )

            @pl.when(jnp.logical_not(local))
            def _():
                remote(
                    final.at[slot], final.at[slot], f_send.at[0, 0], f_recv.at[slot], partner_x
                ).wait_recv()

            total = total + final[slot]
        out[0, 8 * row : 8 * row + 8, :] = total[:, :EIG]
        out[1, 8 * row : 8 * row + 8, :] = total[:, EIG:]

    for copy in eig_copy:
        copy.wait_send()

    @pl.loop(1, STRIPS)
    def _(k):
        a_copy(1, (me + k) % STRIPS).wait_send()

    for which in range(SETS):
        for step in (1, 2, 3):
            x_copy(which, step).wait_send()

    @pl.loop(0, BANDS)
    def _(block):
        @pl.loop(1, 8)
        def _(k):
            r_copy(block, (low + k) % 8).wait_send()

        for q in range(2):
            @pl.when(jnp.logical_not(here(block, q)))
            def _():
                f_copy(block, q).wait_send()


def run(g_cell, pairs, occ, emp, eigvecs):
    t1, t2 = z_tables()
    vmem = pl.BlockSpec(memory_space=pltpu.VMEM)
    anywhere = pl.BlockSpec(memory_space=pl.ANY)
    dma = pltpu.SemaphoreType.DMA
    return pl.pallas_call(
        kernel,
        out_shape=jax.ShapeDtypeStruct((2, 16, EIG), F32),
        in_specs=[pl.BlockSpec(memory_space=pltpu.SMEM), anywhere, vmem, vmem, vmem, vmem, anywhere],
        out_specs=vmem,
        scratch_shapes=[
            pltpu.VMEM((SETS, 8, LANES), jnp.int32),
            pltpu.VMEM((N * N, LANES), F32),
            pltpu.VMEM((33, 2 * N, LANES), F32),
            pltpu.VMEM((5, 8, 2, 8, LANES), F32),
            pltpu.VMEM((SETS, STRIPS, 2, 2 * N, LANES), BF16),
            pltpu.VMEM((SETS, STRIPS, 2, 2 * N, LANES), BF16),
            pltpu.VMEM((CELLS, LANES), F32),
            pltpu.VMEM((4, 8, 2, 16, LANES), F32),
            pltpu.VMEM((G, LANES), F32),
            pltpu.VMEM((SETS, G, LANES), BF16),
            pltpu.VMEM((SETS, XS, ROWS, LANES), BF16),
            pltpu.VMEM((ROWS, 4 * EIG), BF16),
            pltpu.VMEM((BANDS, PAIRS, 4 * EIG), F32),
            pltpu.VMEM((8, BANDS, 8, 4 * EIG), F32),
            pltpu.VMEM((BANDS, 8, 4 * EIG), F32),
            pltpu.VMEM((16, 8, 2 * EIG), F32),
            dma((2,)),
            dma((SETS, STRIPS)),
            dma((SETS, STRIPS)),
            dma((4,)),
            dma((2,)),
            dma((2,)),
            dma((SETS, 3)),
            dma((SETS, 3)),
            dma((BANDS, 8)),
            dma((8, BANDS)),
            dma((BANDS, 2)),
            dma((16,)),
        ],
        compiler_params=pltpu.CompilerParams(
            collective_id=0, has_side_effects=True, vmem_limit_bytes=VMEM_LIMIT
        ),
        name="projections",
    )(g_cell, pairs, occ, emp, jnp.asarray(t1), jnp.asarray(t2), eigvecs)


def shards(occupied, empty, pair_occ, pair_emp, g_cell, eigvecs):
    occ = jnp.transpose(occupied, (1, 2, 3, 0)).reshape(2, N * N, LANES)
    emp = jnp.transpose(empty, (1, 2, 3, 0)).reshape(2, N * N, LANES)
    rows = [jnp.concatenate([pair_occ, pair_occ]), jnp.concatenate([pair_emp, pair_emp])]
    pairs = jnp.stack(rows + [jnp.zeros_like(rows[0])] * 6)
    return run(g_cell, pairs, occ, emp, eigvecs)


def solution(mesh):
    in_specs = (
        P(None, "grid", None, None),
        P(None, "grid", None, None),
        P("band"),
        P("band"),
        P("grid"),
        P(None, "grid", "band"),
    )
    out_specs = P(None, "grid", "band")
    return jax.shard_map(shards, mesh=mesh, in_specs=in_specs, out_specs=out_specs, check_vma=False)
```

```python
import math

import jax
import jax.numpy as jnp
import ml_dtypes
import numpy as np
from jax import lax
from jax.experimental import pallas as pl
from jax.experimental.pallas import tpu as pltpu
from jax.sharding import PartitionSpec as P

N = 64
LANES = 128
PAIRS = 64
STRIPS = 32
BANDS = 8
CELLS = 8192
G = 3840
EIG = 256
ROWS = G // 2
XS = 4
SETS = 2
MESH = pl.DeviceIdType.MESH
F32 = jnp.float32
BF16 = jnp.bfloat16
VMEM_LIMIT = 56 * 1024 * 1024
HALF = math.sqrt(0.5)


def cadd(a, b):
    return (a[0] + b[0], a[1] + b[1])


def csub(a, b):
    return (a[0] - b[0], a[1] - b[1])


def turn(a, k, length):
    k = k % length
    if k == 0:
        return a
    if 4 * k == length:
        return (a[1], -a[0])
    if 2 * k == length:
        return (-a[0], -a[1])
    if 4 * k == 3 * length:
        return (-a[1], a[0])
    if 8 * k == length:
        return ((a[0] + a[1]) * HALF, (a[1] - a[0]) * HALF)
    if 8 * k == 3 * length:
        return ((a[1] - a[0]) * HALF, (a[0] + a[1]) * (-HALF))
    c, s = math.cos(2 * math.pi * k / length), math.sin(2 * math.pi * k / length)
    return (a[0] * c + a[1] * s, a[1] * c - a[0] * s)


def fft4(x):
    a, b, c, d = cadd(x[0], x[2]), csub(x[0], x[2]), cadd(x[1], x[3]), csub(x[1], x[3])
    return [cadd(a, c), (b[0] + d[1], b[1] - d[0]), csub(a, c), (b[0] - d[1], b[1] + d[0])]


def fft8(x):
    even, odd = fft4(x[0::2]), fft4(x[1::2])
    odd = [turn(odd[k], k, 8) for k in range(4)]
    return [cadd(even[k], odd[k]) for k in range(4)] + [csub(even[k], odd[k]) for k in range(4)]


def rfft8(x):
    def four(v):
        a, b, c, d = v[0] + v[2], v[0] - v[2], v[1] + v[3], v[1] - v[3]
        return a + c, (b, -d), a - c

    e0, e1, e2 = four(x[0::2])
    o0, o1, o2 = four(x[1::2])
    o1 = turn(o1, 1, 8)
    low = csub(e1, o1)
    return [e0 + o0, cadd(e1, o1), (e2, -o2), (low[0], -low[1]), e0 - o0]


def z_tables():
    index = np.arange(N)
    angle = (index[:, None] * index[None, :] % N) * (2 * np.pi / N)
    c, s = np.cos(angle) / 512.0, np.sin(angle) / 512.0
    table = np.block([[c, s], [-s, c], [c, -s], [-s, -c]]).astype(np.float32)
    high = table.astype(ml_dtypes.bfloat16)
    low = (table - high.astype(np.float32)).astype(ml_dtypes.bfloat16)
    return np.concatenate([high, high], axis=1), low


def split(value):
    high = value.astype(BF16)
    return high, (value - high.astype(F32)).astype(BF16)


def dot(a, b):
    return jnp.dot(a, b, preferred_element_type=F32)


def one_hot(row):
    r = lax.broadcasted_iota(jnp.int32, (2 * LANES, LANES), 0)
    lane = lax.broadcasted_iota(jnp.int32, (2 * LANES, LANES), 1)
    hit = (r % LANES == row) & (r // LANES == lane // PAIRS)
    return jnp.where(hit, 1.0, 0.0).astype(BF16)


def density(occ_ref, emp_ref, pairs, dens):
    pick_occ, pick_emp = one_hot(pairs[0:1, :]), one_hot(pairs[1:2, :])
    rows = 512

    @pl.loop(0, N * N // rows)
    def _(step):
        at = pl.ds(pl.multiple_of(step * rows, rows), rows)
        occ = jnp.concatenate([occ_ref[0, at, :], occ_ref[1, at, :]], axis=1)
        emp = jnp.concatenate([emp_ref[0, at, :], emp_ref[1, at, :]], axis=1)
        dens[at, :] = dot(occ, pick_occ) * dot(emp, pick_emp)


def transform_y(dens, spec, work):
    @pl.loop(0, 8)
    def _(tile):
        at = pl.multiple_of(tile * 8, 8)
        for n2 in range(8):
            outs = rfft8([dens[pl.ds((8 * n1 + n2) * N + at, 8), :] for n1 in range(8)])
            work[0, n2, 0] = outs[0]
            for k1 in (1, 2, 3):
                re, im = turn(outs[k1], n2 * k1, 64)
                work[k1, n2, 0] = re
                work[k1, n2, 1] = im
            angle = 2 * math.pi * n2 * 4 / 64
            work[4, n2, 0] = outs[4] * math.cos(angle)
            work[4, n2, 1] = outs[4] * (-math.sin(angle))
        outs = rfft8([work[0, n2, 0] for n2 in range(8)])
        zero = jnp.zeros_like(outs[0])
        for k2 in range(5):
            re, im = (outs[k2], zero) if k2 in (0, 4) else outs[k2]
            spec[8 * k2, pl.ds(at, 8), :] = re
            spec[8 * k2, pl.ds(N + at, 8), :] = im
        for k1 in (1, 2, 3, 4):
            outs = fft8([(work[k1, n2, 0], work[k1, n2, 1]) for n2 in range(8)])
            for k2 in range(8 if k1 < 4 else 4):
                ky = k1 + 8 * k2
                re, im = outs[k2]
                if ky > 32:
                    ky, im = 64 - ky, -im
                spec[ky, pl.ds(at, 8), :] = re
                spec[ky, pl.ds(N + at, 8), :] = im


def transform_x(recv, cells, work):
    lane = lax.broadcasted_iota(jnp.int32, (8, LANES), 1)
    left = lane < PAIRS

    @pl.loop(0, 2 * 4)
    def _(tile):
        kyl = tile // 4
        at = pl.multiple_of((tile % 4) * 16, 16)
        for n2 in range(8):
            outs = fft4(
                [
                    (
                        recv[8 * n1 + n2, kyl, pl.ds(at, 16), :].astype(F32),
                        recv[8 * n1 + n2, kyl, pl.ds(N + at, 16), :].astype(F32),
                    )
                    for n1 in range(4)
                ]
            )
            for k1 in range(4):
                re, im = turn(outs[k1], n2 * k1, 32)
                work[k1, n2, 0] = re
                work[k1, n2, 1] = im
        for half in range(2):
            rows = slice(8 * half, 8 * half + 8)
            for k1 in range(4):
                outs = fft8([(work[k1, n2, 0, rows], work[k1, n2, 1, rows]) for n2 in range(8)])
                for k2 in range(8):
                    kx = k1 + 4 * k2
                    re, im = outs[k2]
                    c = jnp.where(left, 1.0, math.cos(2 * math.pi * kx / 64))
                    s = jnp.where(left, 0.0, math.sin(2 * math.pi * kx / 64))
                    re, im = re * c + im * s, im * c - re * s
                    even = jnp.where(left, re, pltpu.roll(im, PAIRS, axis=1))
                    odd = jnp.where(left, pltpu.roll(re, PAIRS, axis=1), im)
                    cell = kyl * N + at + 8 * half
                    cells[pl.ds(kx * LANES + cell, 8), :] = even + odd
                    cells[pl.ds((kx + 32) * LANES + cell, 8), :] = even - odd


def pick(cell_ref, cells, rows, out, part):
    block = 128

    @pl.loop(0, ROWS // block)
    def _(step):
        at = pl.multiple_of(part * ROWS + step * block, block)
        for i in range(block):
            rows[i : i + 1, :] = cells[pl.ds(cell_ref[at + i], 1), :]
        out[pl.ds(at, block), :] = rows[...].astype(BF16)


def kernel(
    cell_ref, pocc_ref, pemp_ref, occ_any, emp_any, t1_ref, t2_ref, eig_ref, out,
    occ_ref, emp_ref, lists, dens, spec, work_y, send, recv, cells, work_x, rows, own, held, eigs, sums, parts,
    done, final0, final1,
    list_sems, a_send, a_recv, local_sems, e_send, e_recv, x_send, x_recv, r_send, r_recv, f_send, f_recv,
):
    band = lax.axis_index("band")
    me = lax.axis_index("grid")
    x, zh = band // 2, band % 2
    zl, low = me // 8, me % 8
    core = me % 2
    z = zh * 4 + zl
    half = x % 2

    def peer(strip):
        steps = (strip // 8 - zl + 4) % 4
        side = (zl // 2 + core + strip) % 2
        away = steps - 4 * (steps // 3) - 4 * side * (steps // 2 - steps // 3)
        return (2 * x + ((z + away + 8) % 8) // 4, strip)

    def along_x(step):
        return (2 * ((x + step) % XS) + zh, me)

    partner_z = (band + 1 - 2 * zh, me)
    beside = [(2 * ((x + 1 - 2 * half) % XS) + zh, me), (2 * ((x + 3 + 2 * half) % XS) + zh, me)]

    barrier = pltpu.get_barrier_semaphore()

    def greet(device):
        pl.semaphore_signal(barrier, inc=1, device_id=device, device_id_type=MESH)

    def remote(src, dst, send_sem, recv_sem, device):
        return pltpu.make_async_remote_copy(
            src_ref=src, dst_ref=dst, send_sem=send_sem, recv_sem=recv_sem, device_id=device, device_id_type=MESH
        )

    slabs = [
        pltpu.make_async_copy(occ_any, occ_ref, local_sems.at[0]),
        pltpu.make_async_copy(emp_any, emp_ref, local_sems.at[1]),
    ]
    own_at = pl.ds(pl.multiple_of(half * ROWS, ROWS), ROWS)
    other_at = pl.ds(pl.multiple_of((1 - half) * ROWS, ROWS), ROWS)
    eig_own = [
        pltpu.make_async_copy(
            eig_ref.at[i, own_at], eigs.at[:, pl.ds(i * EIG, EIG)], local_sems.at[2 + i]
        )
        for i in range(2)
    ]
    for copy in slabs + eig_own:
        copy.start()

    @pl.loop(1, STRIPS)
    def _(k):
        greet(peer((me + k) % STRIPS))

    greet(partner_z)
    for step in (1, 2, 3):
        greet(along_x(step))

    @pl.loop(0, 8)
    def _(k):
        source = (k // 2) * 8 + 2 * (low % 4) + k % 2
        greet((beside[0][0], source))
        greet((beside[1][0], source))

        @pl.when(source != me)
        def _():
            greet((band, source))

    mine = jnp.where(jnp.logical_or(low == 0, low == 7), 1, 0)

    def prepare(which):
        density(occ_ref, emp_ref, lists[which], dens)
        transform_y(dens, spec.at[which], work_y)

    lists[zh, 0:1, :] = jnp.concatenate([pocc_ref[...], pocc_ref[...]], axis=1)
    lists[zh, 1:2, :] = jnp.concatenate([pemp_ref[...], pemp_ref[...]], axis=1)
    lists[zh, 2:8, :] = jnp.zeros((6, LANES), jnp.int32)
    for copy in slabs:
        copy.wait()
    prepare(zh)
    pl.semaphore_wait(barrier, 31 + 1 + 3 + 24 - mine)

    list_copy = remote(lists.at[zh], lists.at[zh], list_sems.at[0], list_sems.at[1], partner_z)
    list_copy.start()
    eig_copy = [
        remote(
            eig_ref.at[i, other_at, pl.ds(k * 128, 128)], eigs.at[:, pl.ds(512 + k * 256 + i * 128, 128)],
            e_send.at[k, i], e_recv.at[k, i], beside[k],
        )
        for k in range(2)
        for i in range(2)
    ]
    for copy in eig_copy:
        copy.start()

    def a_copy(which, strip):
        return remote(
            send.at[which, strip], recv.at[which, me], a_send.at[which, strip], a_recv.at[which, me], peer(strip)
        )

    def planes(which):
        def start(strip):
            @pl.when(strip != me)
            def _():
                if which:
                    a_copy(0, strip).wait_send()
                a_copy(which, strip).start()

        @pl.loop(0, 16)
        def _(step):
            j = (me + step) % 16
            h0, l0 = split(spec[which, 2 * j])
            h1, l1 = split(spec[which, 2 * j + 1])
            high = jnp.concatenate([h0, h1], axis=1)
            low_part = jnp.concatenate([l0, l1], axis=1)
            both = dot(t1_ref[...], jnp.concatenate([high, low_part], axis=0)) + dot(t2_ref[...], high)
            both = both.astype(BF16)
            send[which, j, 0] = both[:LANES, :LANES]
            send[which, j, 1] = both[:LANES, LANES:]
            start(j)

            @pl.when(j > 0)
            def _():
                send[which, 32 - j, 0] = both[LANES:, :LANES]

            send[which, 31 - j, 1] = both[LANES:, LANES:]

        h0, l0 = split(spec[which, 32])
        one = dot(t1_ref[:LANES, :], jnp.concatenate([h0, l0], axis=0)) + dot(t2_ref[:LANES, :], h0)
        send[which, 16, 0] = one.astype(BF16)

        @pl.loop(0, 16)
        def _(step):
            start(16 + (me + step) % 16)

        copy = pltpu.make_async_copy(send.at[which, me], recv.at[which, me], local_sems.at[4])
        copy.start()
        copy.wait()

    def x_copy(which, step):
        part = half if step == 2 else 1 - half
        return remote(
            own.at[which, pl.ds(pl.multiple_of(part * ROWS, ROWS), ROWS)], held.at[which, x],
            x_send.at[which, step - 1], x_recv.at[which, step - 1], along_x(step),
        )

    def columns(which):
        @pl.loop(1, STRIPS)
        def _(k):
            source = (me + k) % STRIPS
            remote(
                send.at[which, source], recv.at[which, source], a_send.at[which, source],
                a_recv.at[which, source], peer(source),
            ).wait_recv()

        transform_x(recv.at[which], cells, work_x)
        pick(cell_ref, cells, rows, own.at[which], 1 - half)
        x_copy(which, 1).start()
        x_copy(which, 3).start()
        pick(cell_ref, cells, rows, own.at[which], half)

    def r_copy(block, to):
        return remote(
            sums.at[block, pl.ds(pl.multiple_of(to * 8, 8), 8)], parts.at[low, block],
            r_send.at[block, to], r_recv.at[low, block], (band, zl * 8 + to),
        )

    def multiply(src, block):
        for q in range(2):
            base = q * 2 * EIG
            part = lax.dot_general(
                src[...], eigs[:, base : base + 2 * EIG], (((0,), (0,)), ((), ())), preferred_element_type=F32
            )
            wide = EIG if q == 0 else EIG // 2
            for at in range(0, 2 * EIG, 2 * wide):
                first, second = slice(at, at + wide), slice(at + wide, at + 2 * wide)
                sums[block, :, base + at : base + at + wide] = part[:PAIRS, first] + part[PAIRS:, second]
                sums[block, :, base + at + wide : base + at + 2 * wide] = part[:PAIRS, second] - part[PAIRS:, first]

        @pl.loop(1, 8)
        def _(k):
            r_copy(block, (low + k) % 8).start()

    def multiply_own(which):
        multiply(own.at[which, own_at], 2 * x + which)

    def multiply_from(which, step):
        x_copy(which, step).wait_recv()
        source = (x - step + XS) % XS
        multiply(held.at[which, source], 2 * source + which)

    def owner(block):
        return (block // 2) * 8 + 4 * (block % 2) + low // 2

    slot = zl * 2 + low % 2

    def f_copy(block, q):
        if q == 0:
            src, dst, to = done.at[block, :, pl.ds(0, 512)], final0.at[slot], band
        else:
            src, dst = done.at[block, :, pl.ds(256 + 256 * q, 256)], final1.at[q - 1, slot]
            to = beside[q - 1][0]
        return remote(src, dst, f_send.at[block, q], f_recv.at[q, slot], (to, owner(block)))

    def reduce(which, first, last):
        @pl.loop(first, last)
        def _(k):
            step = k + k // 2 - 2 * (k // 3)
            block = 2 * ((x + XS - step) % XS) + which
            mine_at = pl.ds(pl.multiple_of(low * 8, 8), 8)

            def add(k, total):
                source = (low + k) % 8
                remote(
                    sums.at[block, mine_at], parts.at[source, block], r_send.at[block, source],
                    r_recv.at[source, block], (band, zl * 8 + source),
                ).wait_recv()
                return total + parts[source, block]

            done[block] = lax.fori_loop(1, 8, add, sums[block, mine_at, :])
            f_copy(block, 1).start()
            f_copy(block, 2).start()
            local = owner(block) == me

            @pl.when(jnp.logical_not(local))
            def _():
                f_copy(block, 0).start()

            @pl.when(local)
            def _():
                final0[slot] = done[block, :, :512]

    @pl.when(zh == 1)
    def _():
        list_copy.wait()
        prepare(0)

    planes(0)

    @pl.when(zh == 0)
    def _():
        list_copy.wait()
        prepare(1)

    planes(1)
    columns(0)
    x_copy(0, 2).start()
    for copy in eig_own:
        copy.wait()
    for copy in eig_copy:
        copy.wait_recv()
    multiply_own(0)
    columns(1)
    multiply_own(1)
    for step in (1, 3, 2):
        multiply_from(0, step)
    x_copy(1, 1).wait_send()
    x_copy(1, 3).wait_send()
    x_copy(1, 2).start()
    multiply_from(1, 1)
    multiply_from(1, 3)
    reduce(0, 0, 4)
    reduce(1, 0, 3)
    multiply_from(1, 2)
    reduce(1, 3, 4)

    for row in range(2):
        total = jnp.zeros((8, 2 * EIG), F32)
        ends = [jnp.zeros((8, EIG), F32)] * 2
        for k in range(4):
            at = 2 * k + row
            local = jnp.logical_and(
                jnp.logical_and(zl == k, low % 2 == row), jnp.logical_or(low == 0, low == 7)
            )

            @pl.when(jnp.logical_not(local))
            def _():
                remote(final0.at[at], final0.at[at], f_send.at[0, 0], f_recv.at[0, at], partner_z).wait_recv()

            total = total + final0[at]
            for q in range(2):
                remote(
                    final1.at[q, at], final1.at[q, at], f_send.at[0, 0], f_recv.at[1 + q, at], partner_z
                ).wait_recv()
                ends[q] = ends[q] + final1[q, at]
        for i in range(2):
            for q in range(2):
                base = i * EIG + q * 128
                out[i, 8 * row : 8 * row + 8, q * 128 : q * 128 + 128] = (
                    total[:, base : base + 128] + ends[q][:, i * 128 : i * 128 + 128]
                )

    for copy in eig_copy:
        copy.wait_send()

    @pl.loop(1, STRIPS)
    def _(k):
        a_copy(1, (me + k) % STRIPS).wait_send()

    for step in (1, 2, 3):
        x_copy(0, step).wait_send()
    x_copy(1, 2).wait_send()

    @pl.loop(0, BANDS)
    def _(block):
        @pl.loop(1, 8)
        def _(k):
            r_copy(block, (low + k) % 8).wait_send()

        f_copy(block, 1).wait_send()
        f_copy(block, 2).wait_send()

        @pl.when(owner(block) != me)
        def _():
            f_copy(block, 0).wait_send()


def run(g_cell, pocc, pemp, occ, emp, eigvecs):
    t1, t2 = z_tables()
    vmem = pl.BlockSpec(memory_space=pltpu.VMEM)
    anywhere = pl.BlockSpec(memory_space=pl.ANY)
    dma = pltpu.SemaphoreType.DMA
    return pl.pallas_call(
        kernel,
        out_shape=jax.ShapeDtypeStruct((2, 16, EIG), F32),
        in_specs=[pl.BlockSpec(memory_space=pltpu.SMEM), vmem, vmem, anywhere, anywhere, vmem, vmem, anywhere],
        out_specs=vmem,
        scratch_shapes=[
            pltpu.VMEM((2, N * N, LANES), BF16),
            pltpu.VMEM((2, N * N, LANES), BF16),
            pltpu.VMEM((SETS, 8, LANES), jnp.int32),
            pltpu.VMEM((N * N, LANES), F32),
            pltpu.VMEM((SETS, 33, 2 * N, LANES), F32),
            pltpu.VMEM((5, 8, 2, 8, LANES), F32),
            pltpu.VMEM((SETS, STRIPS, 2, 2 * N, LANES), BF16),
            pltpu.VMEM((SETS, STRIPS, 2, 2 * N, LANES), BF16),
            pltpu.VMEM((CELLS, LANES), F32),
            pltpu.VMEM((4, 8, 2, 16, LANES), F32),
            pltpu.VMEM((128, LANES), F32),
            pltpu.VMEM((SETS, G, LANES), BF16),
            pltpu.VMEM((SETS, XS, ROWS, LANES), BF16),
            pltpu.VMEM((ROWS, 4 * EIG), BF16),
            pltpu.VMEM((BANDS, PAIRS, 4 * EIG), F32),
            pltpu.VMEM((8, BANDS, 8, 4 * EIG), F32),
            pltpu.VMEM((BANDS, 8, 4 * EIG), F32),
            pltpu.VMEM((8, 8, 2 * EIG), F32),
            pltpu.VMEM((2, 8, 8, EIG), F32),
            dma((2,)),
            dma((SETS, STRIPS)),
            dma((SETS, STRIPS)),
            dma((5,)),
            dma((2, 2)),
            dma((2, 2)),
            dma((SETS, 3)),
            dma((SETS, 3)),
            dma((BANDS, 8)),
            dma((8, BANDS)),
            dma((BANDS, 3)),
            dma((3, 8)),
        ],
        compiler_params=pltpu.CompilerParams(
            collective_id=0, has_side_effects=True, vmem_limit_bytes=VMEM_LIMIT
        ),
        name="projections",
    )(g_cell, pocc, pemp, occ, emp, jnp.asarray(t1), jnp.asarray(t2), eigvecs)


def shards(occupied, empty, pair_occ, pair_emp, g_cell, eigvecs):
    occ = jnp.transpose(occupied, (1, 2, 3, 0)).reshape(2, N * N, LANES)
    emp = jnp.transpose(empty, (1, 2, 3, 0)).reshape(2, N * N, LANES)
    return run(g_cell, pair_occ.reshape(1, PAIRS), pair_emp.reshape(1, PAIRS), occ, emp, eigvecs)


def solution(mesh):
    in_specs = (
        P(None, "grid", None, None),
        P(None, "grid", None, None),
        P("band"),
        P("band"),
        P("grid"),
        P(None, "grid", "band"),
    )
    out_specs = P(None, "grid", "band")
    return jax.shard_map(shards, mesh=mesh, in_specs=in_specs, out_specs=out_specs, check_vma=False)
```

```python
import math

import jax
import jax.numpy as jnp
import ml_dtypes
import numpy as np
from jax import lax
from jax.experimental import pallas as pl
from jax.experimental.pallas import tpu as pltpu
from jax.sharding import PartitionSpec as P

N = 64
LANES = 128
PAIRS = 64
STRIPS = 32
BANDS = 8
CELLS = 8192
G = 3840
EIG = 256
ROWS = G // 2
XS = 4
SETS = 2
MESH = pl.DeviceIdType.MESH
F32 = jnp.float32
BF16 = jnp.bfloat16
VMEM_LIMIT = 56 * 1024 * 1024
HALF = math.sqrt(0.5)


def cadd(a, b):
    return (a[0] + b[0], a[1] + b[1])


def csub(a, b):
    return (a[0] - b[0], a[1] - b[1])


def turn(a, k, length):
    k = k % length
    if k == 0:
        return a
    if 4 * k == length:
        return (a[1], -a[0])
    if 2 * k == length:
        return (-a[0], -a[1])
    if 4 * k == 3 * length:
        return (-a[1], a[0])
    if 8 * k == length:
        return ((a[0] + a[1]) * HALF, (a[1] - a[0]) * HALF)
    if 8 * k == 3 * length:
        return ((a[1] - a[0]) * HALF, (a[0] + a[1]) * (-HALF))
    c, s = math.cos(2 * math.pi * k / length), math.sin(2 * math.pi * k / length)
    return (a[0] * c + a[1] * s, a[1] * c - a[0] * s)


def fft4(x):
    a, b, c, d = cadd(x[0], x[2]), csub(x[0], x[2]), cadd(x[1], x[3]), csub(x[1], x[3])
    return [cadd(a, c), (b[0] + d[1], b[1] - d[0]), csub(a, c), (b[0] - d[1], b[1] + d[0])]


def fft8(x):
    even, odd = fft4(x[0::2]), fft4(x[1::2])
    odd = [turn(odd[k], k, 8) for k in range(4)]
    return [cadd(even[k], odd[k]) for k in range(4)] + [csub(even[k], odd[k]) for k in range(4)]


def rfft8(x):
    def four(v):
        a, b, c, d = v[0] + v[2], v[0] - v[2], v[1] + v[3], v[1] - v[3]
        return a + c, (b, -d), a - c

    e0, e1, e2 = four(x[0::2])
    o0, o1, o2 = four(x[1::2])
    o1 = turn(o1, 1, 8)
    low = csub(e1, o1)
    return [e0 + o0, cadd(e1, o1), (e2, -o2), (low[0], -low[1]), e0 - o0]


def z_tables():
    index = np.arange(N)
    angle = (index[:, None] * index[None, :] % N) * (2 * np.pi / N)
    c, s = np.cos(angle) / 512.0, np.sin(angle) / 512.0
    table = np.block([[c, s], [-s, c], [c, -s], [-s, -c]]).astype(np.float32)
    high = table.astype(ml_dtypes.bfloat16)
    low = (table - high.astype(np.float32)).astype(ml_dtypes.bfloat16)
    return np.concatenate([high, high], axis=1), low


def split(value):
    high = value.astype(BF16)
    return high, (value - high.astype(F32)).astype(BF16)


def dot(a, b):
    return jnp.dot(a, b, preferred_element_type=F32)


def one_hot(row):
    r = lax.broadcasted_iota(jnp.int32, (2 * LANES, LANES), 0)
    lane = lax.broadcasted_iota(jnp.int32, (2 * LANES, LANES), 1)
    hit = (r % LANES == row) & (r // LANES == lane // PAIRS)
    return jnp.where(hit, 1.0, 0.0).astype(BF16)


def density(occ_ref, emp_ref, pairs, dens):
    pick_occ, pick_emp = one_hot(pairs[0:1, :]), one_hot(pairs[1:2, :])
    rows = 512

    @pl.loop(0, N * N // rows)
    def _(step):
        at = pl.ds(pl.multiple_of(step * rows, rows), rows)
        occ = jnp.concatenate([occ_ref[0, at, :], occ_ref[1, at, :]], axis=1)
        emp = jnp.concatenate([emp_ref[0, at, :], emp_ref[1, at, :]], axis=1)
        dens[at, :] = dot(occ, pick_occ) * dot(emp, pick_emp)


def transform_y(dens, spec, work):
    @pl.loop(0, 8)
    def _(tile):
        at = pl.multiple_of(tile * 8, 8)
        for n2 in range(8):
            outs = rfft8([dens[pl.ds((8 * n1 + n2) * N + at, 8), :] for n1 in range(8)])
            work[0, n2, 0] = outs[0]
            for k1 in (1, 2, 3):
                re, im = turn(outs[k1], n2 * k1, 64)
                work[k1, n2, 0] = re
                work[k1, n2, 1] = im
            angle = 2 * math.pi * n2 * 4 / 64
            work[4, n2, 0] = outs[4] * math.cos(angle)
            work[4, n2, 1] = outs[4] * (-math.sin(angle))
        outs = rfft8([work[0, n2, 0] for n2 in range(8)])
        zero = jnp.zeros_like(outs[0])
        for k2 in range(5):
            re, im = (outs[k2], zero) if k2 in (0, 4) else outs[k2]
            spec[8 * k2, pl.ds(at, 8), :] = re
            spec[8 * k2, pl.ds(N + at, 8), :] = im
        for k1 in (1, 2, 3, 4):
            outs = fft8([(work[k1, n2, 0], work[k1, n2, 1]) for n2 in range(8)])
            for k2 in range(8 if k1 < 4 else 4):
                ky = k1 + 8 * k2
                re, im = outs[k2]
                if ky > 32:
                    ky, im = 64 - ky, -im
                spec[ky, pl.ds(at, 8), :] = re
                spec[ky, pl.ds(N + at, 8), :] = im


def transform_x(recv, cells, work):
    lane = lax.broadcasted_iota(jnp.int32, (8, LANES), 1)
    left = lane < PAIRS

    @pl.loop(0, 2 * 4)
    def _(tile):
        kyl = tile // 4
        at = pl.multiple_of((tile % 4) * 16, 16)
        for n2 in range(8):
            outs = fft4(
                [
                    (
                        recv[8 * n1 + n2, kyl, pl.ds(at, 16), :].astype(F32),
                        recv[8 * n1 + n2, kyl, pl.ds(N + at, 16), :].astype(F32),
                    )
                    for n1 in range(4)
                ]
            )
            for k1 in range(4):
                re, im = turn(outs[k1], n2 * k1, 32)
                work[k1, n2, 0] = re
                work[k1, n2, 1] = im
        for half in range(2):
            rows = slice(8 * half, 8 * half + 8)
            for k1 in range(4):
                outs = fft8([(work[k1, n2, 0, rows], work[k1, n2, 1, rows]) for n2 in range(8)])
                for k2 in range(8):
                    kx = k1 + 4 * k2
                    re, im = outs[k2]
                    c = jnp.where(left, 1.0, math.cos(2 * math.pi * kx / 64))
                    s = jnp.where(left, 0.0, math.sin(2 * math.pi * kx / 64))
                    re, im = re * c + im * s, im * c - re * s
                    even = jnp.where(left, re, pltpu.roll(im, PAIRS, axis=1))
                    odd = jnp.where(left, pltpu.roll(re, PAIRS, axis=1), im)
                    cell = kyl * N + at + 8 * half
                    cells[pl.ds(kx * LANES + cell, 8), :] = even + odd
                    cells[pl.ds((kx + 32) * LANES + cell, 8), :] = even - odd


def pick(cell_ref, cells, rows, out, part):
    block = 128

    @pl.loop(0, ROWS // block)
    def _(step):
        at = pl.multiple_of(part * ROWS + step * block, block)
        for i in range(block):
            rows[i : i + 1, :] = cells[pl.ds(cell_ref[at + i], 1), :]
        out[pl.ds(at, block), :] = rows[...].astype(BF16)


def kernel(
    cell_ref, pocc_ref, pemp_ref, occ_any, emp_any, t1_ref, t2_ref, eig_ref, out,
    occ_ref, emp_ref, lists, dens, spec, work_y, send, recv, cells, work_x, rows, own, held, eigs, sums, parts,
    done, final0, final1,
    list_sems, a_send, a_recv, local_sems, e_send, e_recv, x_send, x_recv, r_send, r_recv, f_send, f_recv,
):
    band = lax.axis_index("band")
    me = lax.axis_index("grid")
    x, zh = band // 2, band % 2
    zl, low = me // 8, me % 8
    core = me % 2
    z = zh * 4 + zl
    half = x % 2

    def peer(strip):
        steps = (strip // 8 - zl + 4) % 4
        side = (zl // 2 + core + strip) % 2
        away = steps - 4 * (steps // 3) - 4 * side * (steps // 2 - steps // 3)
        return (2 * x + ((z + away + 8) % 8) // 4, strip)

    def along_x(step):
        return (2 * ((x + step) % XS) + zh, me)

    partner_z = (band + 1 - 2 * zh, me)
    beside = [(2 * ((x + 1 - 2 * half) % XS) + zh, me), (2 * ((x + 3 + 2 * half) % XS) + zh, me)]

    barrier = pltpu.get_barrier_semaphore()

    def greet(device):
        pl.semaphore_signal(barrier, inc=1, device_id=device, device_id_type=MESH)

    def remote(src, dst, send_sem, recv_sem, device):
        return pltpu.make_async_remote_copy(
            src_ref=src, dst_ref=dst, send_sem=send_sem, recv_sem=recv_sem, device_id=device, device_id_type=MESH
        )

    slabs = [
        pltpu.make_async_copy(occ_any, occ_ref, local_sems.at[0]),
        pltpu.make_async_copy(emp_any, emp_ref, local_sems.at[1]),
    ]
    own_at = pl.ds(pl.multiple_of(half * ROWS, ROWS), ROWS)
    other_at = pl.ds(pl.multiple_of((1 - half) * ROWS, ROWS), ROWS)
    eig_own = [
        pltpu.make_async_copy(
            eig_ref.at[i, own_at], eigs.at[:, pl.ds(i * EIG, EIG)], local_sems.at[2 + i]
        )
        for i in range(2)
    ]
    for copy in slabs + eig_own:
        copy.start()

    @pl.loop(1, STRIPS)
    def _(k):
        greet(peer((me + k) % STRIPS))

    greet(partner_z)
    for step in (1, 2, 3):
        greet(along_x(step))

    @pl.loop(0, 8)
    def _(k):
        source = (k // 2) * 8 + 2 * (low % 4) + k % 2
        greet((beside[0][0], source))
        greet((beside[1][0], source))

        @pl.when(source != me)
        def _():
            greet((band, source))

    mine = jnp.where(jnp.logical_or(low == 0, low == 7), 1, 0)

    def prepare(which):
        density(occ_ref, emp_ref, lists[which], dens)
        transform_y(dens, spec.at[which], work_y)

    lists[zh, 0:1, :] = jnp.concatenate([pocc_ref[...], pocc_ref[...]], axis=1)
    lists[zh, 1:2, :] = jnp.concatenate([pemp_ref[...], pemp_ref[...]], axis=1)
    lists[zh, 2:8, :] = jnp.zeros((6, LANES), jnp.int32)
    for copy in slabs:
        copy.wait()
    prepare(zh)
    pl.semaphore_wait(barrier, 31 + 1 + 3 + 24 - mine)

    list_copy = remote(lists.at[zh], lists.at[zh], list_sems.at[0], list_sems.at[1], partner_z)
    list_copy.start()
    eig_copy = [
        remote(
            eig_ref.at[i, other_at, pl.ds(k * 128, 128)], eigs.at[:, pl.ds(512 + k * 256 + i * 128, 128)],
            e_send.at[k, i], e_recv.at[k, i], beside[k],
        )
        for k in range(2)
        for i in range(2)
    ]
    for copy in eig_copy:
        copy.start()

    def a_copy(phase, strip):
        device = peer(strip)
        pairs = (device[0] + phase) % 2
        return remote(
            send.at[pairs, strip], recv.at[phase, me], a_send.at[STRIPS if phase else strip], a_recv.at[phase], device
        )

    def planes(which, near):
        def start(strip):
            same = peer(strip)[0] % 2 == zh

            @pl.when(jnp.logical_and(same, strip != me) if near else jnp.logical_not(same))
            def _():
                a_copy(0, strip).start()

        @pl.loop(0, 16)
        def _(step):
            j = (me + step) % 16
            h0, l0 = split(spec[which, 2 * j])
            h1, l1 = split(spec[which, 2 * j + 1])
            high = jnp.concatenate([h0, h1], axis=1)
            low_part = jnp.concatenate([l0, l1], axis=1)
            both = dot(t1_ref[...], jnp.concatenate([high, low_part], axis=0)) + dot(t2_ref[...], high)
            both = both.astype(BF16)
            send[which, j, 0] = both[:LANES, :LANES]
            send[which, j, 1] = both[:LANES, LANES:]
            start(j)
            send[which, 31 - j, 1] = both[LANES:, LANES:]

            @pl.when(j > 0)
            def _():
                send[which, 32 - j, 0] = both[LANES:, :LANES]

                @pl.when(step > 0)
                def _():
                    start(32 - j)

        h0, l0 = split(spec[which, 32])
        one = dot(t1_ref[:LANES, :], jnp.concatenate([h0, l0], axis=0)) + dot(t2_ref[:LANES, :], h0)
        send[which, 16, 0] = one.astype(BF16)
        start(16)

        @pl.when(me % 16 > 0)
        def _():
            start(32 - me % 16)

    def x_copy(which, step):
        part = half if step == 2 else 1 - half
        return remote(
            own.at[which, pl.ds(pl.multiple_of(part * ROWS, ROWS), ROWS)], held.at[which, x],
            x_send.at[which, step - 1], x_recv.at[which, step - 1], along_x(step),
        )

    def columns(which):
        got = recv.at[which, pl.ds(0, STRIPS - 1)]
        remote(got, got, a_send.at[0], a_recv.at[which], partner_z).wait_recv()
        transform_x(recv.at[which], cells, work_x)
        pick(cell_ref, cells, rows, own.at[which], 1 - half)
        x_copy(which, 1).start()
        x_copy(which, 3).start()
        pick(cell_ref, cells, rows, own.at[which], half)

    def r_copy(block, to):
        return remote(
            sums.at[block, pl.ds(pl.multiple_of(to * 8, 8), 8)], parts.at[block, low],
            r_send.at[0], r_recv.at[block], (band, zl * 8 + to),
        )

    def multiply(src, block):
        for q in range(2):
            base = q * 2 * EIG
            part = lax.dot_general(
                src[...], eigs[:, base : base + 2 * EIG], (((0,), (0,)), ((), ())), preferred_element_type=F32
            )
            wide = EIG if q == 0 else EIG // 2
            for at in range(0, 2 * EIG, 2 * wide):
                first, second = slice(at, at + wide), slice(at + wide, at + 2 * wide)
                sums[block, :, base + at : base + at + wide] = part[:PAIRS, first] + part[PAIRS:, second]
                sums[block, :, base + at + wide : base + at + 2 * wide] = part[:PAIRS, second] - part[PAIRS:, first]

        @pl.loop(1, 8)
        def _(k):
            r_copy(block, (low + k) % 8).start()

    def multiply_own(which):
        multiply(own.at[which, own_at], 2 * x + (zh + which) % 2)

    def multiply_from(which, step):
        x_copy(which, step).wait_recv()
        source = (x - step + XS) % XS
        multiply(held.at[which, source], 2 * source + (zh + which) % 2)

    def owner(block):
        return (block // 2) * 8 + 4 * (block % 2) + low // 2

    slot = zl * 2 + low % 2

    def f_copy(block, q):
        if q == 0:
            src, dst, to = done.at[block, :, pl.ds(0, 512)], final0.at[slot], band
        else:
            src, dst = done.at[block, :, pl.ds(256 + 256 * q, 256)], final1.at[q - 1, slot]
            to = beside[q - 1][0]
        return remote(src, dst, f_send.at[min(q, 1)], f_recv.at[min(q, 1)], (to, owner(block)))

    def reduce(which, first, last):
        @pl.loop(first, last)
        def _(k):
            step = k + k // 2 - 2 * (k // 3)
            block = 2 * ((x + XS - step) % XS) + (zh + which) % 2
            mine_at = pl.ds(pl.multiple_of(low * 8, 8), 8)

            got = parts.at[block, pl.ds(0, 7)]
            remote(got, got, r_send.at[0], r_recv.at[block], partner_z).wait_recv()
            total = sums[block, mine_at, :]
            for i in range(1, 8):
                total = total + parts[block, (low + i) % 8]
            done[block] = total
            f_copy(block, 1).start()
            f_copy(block, 2).start()
            local = owner(block) == me

            @pl.when(jnp.logical_not(local))
            def _():
                f_copy(block, 0).start()

            @pl.when(local)
            def _():
                final0[slot] = done[block, :, :512]

    planes(zh, True)
    list_copy.wait()
    prepare(1 - zh)
    planes(1 - zh, False)
    stay = [
        pltpu.make_async_copy(send.at[(zh + phase) % 2, me], recv.at[phase, me], local_sems.at[4 + phase])
        for phase in range(2)
    ]
    for copy in stay:
        copy.start()

    @pl.loop(1, STRIPS)
    def _(k):
        strip = (me + k // 2 + 16 * (k % 2)) % STRIPS
        a_copy(1, strip).start()

    for copy in stay:
        copy.wait()
    columns(0)
    x_copy(0, 2).start()
    for copy in eig_own:
        copy.wait()
    for copy in eig_copy:
        copy.wait_recv()
    multiply_own(0)
    columns(1)
    x_copy(1, 2).start()
    multiply_own(1)
    for step in (1, 3, 2):
        multiply_from(0, step)
    reduce(0, 0, 4)
    multiply_from(1, 1)
    multiply_from(1, 3)
    multiply_from(1, 2)
    reduce(1, 0, 4)

    def finish(way):
        @pl.when(mine == 1)
        def _():
            way(remote(final0.at[pl.ds(0, 7)], final0.at[pl.ds(0, 7)], f_send.at[0], f_recv.at[0], partner_z))

        @pl.when(mine == 0)
        def _():
            way(remote(final0, final0, f_send.at[0], f_recv.at[0], partner_z))

        way(remote(final1, final1, f_send.at[1], f_recv.at[1], partner_z))

    finish(lambda copy: copy.wait_recv())
    for row in range(2):
        total = jnp.zeros((8, 2 * EIG), F32)
        ends = [jnp.zeros((8, EIG), F32)] * 2
        for k in range(4):
            total = total + final0[2 * k + row]
            for q in range(2):
                ends[q] = ends[q] + final1[q, 2 * k + row]
        for i in range(2):
            for q in range(2):
                base = i * EIG + q * 128
                out[i, 8 * row : 8 * row + 8, q * 128 : q * 128 + 128] = (
                    total[:, base : base + 128] + ends[q][:, i * 128 : i * 128 + 128]
                )

    for copy in eig_copy:
        copy.wait_send()

    @pl.loop(1, STRIPS)
    def _(k):
        a_copy(0, (me + k) % STRIPS).wait_send()

    gone = recv.at[0, pl.ds(0, STRIPS - 1)]
    remote(gone, gone, a_send.at[STRIPS], a_recv.at[0], partner_z).wait_send()
    for step in (1, 2, 3):
        x_copy(0, step).wait_send()
    for step in (1, 2, 3):
        x_copy(1, step).wait_send()
    gone = parts.at[pl.ds(0, 7)]
    remote(gone, gone, r_send.at[0], r_recv.at[0], partner_z).wait_send()
    finish(lambda copy: copy.wait_send())


def run(g_cell, pocc, pemp, occ, emp, eigvecs):
    t1, t2 = z_tables()
    vmem = pl.BlockSpec(memory_space=pltpu.VMEM)
    anywhere = pl.BlockSpec(memory_space=pl.ANY)
    dma = pltpu.SemaphoreType.DMA
    return pl.pallas_call(
        kernel,
        out_shape=jax.ShapeDtypeStruct((2, 16, EIG), F32),
        in_specs=[pl.BlockSpec(memory_space=pltpu.SMEM), vmem, vmem, anywhere, anywhere, vmem, vmem, anywhere],
        out_specs=vmem,
        scratch_shapes=[
            pltpu.VMEM((2, N * N, LANES), BF16),
            pltpu.VMEM((2, N * N, LANES), BF16),
            pltpu.VMEM((SETS, 8, LANES), jnp.int32),
            pltpu.VMEM((N * N, LANES), F32),
            pltpu.VMEM((SETS, 33, 2 * N, LANES), F32),
            pltpu.VMEM((5, 8, 2, 8, LANES), F32),
            pltpu.VMEM((SETS, STRIPS, 2, 2 * N, LANES), BF16),
            pltpu.VMEM((SETS, STRIPS, 2, 2 * N, LANES), BF16),
            pltpu.VMEM((CELLS, LANES), F32),
            pltpu.VMEM((4, 8, 2, 16, LANES), F32),
            pltpu.VMEM((128, LANES), F32),
            pltpu.VMEM((SETS, G, LANES), BF16),
            pltpu.VMEM((SETS, XS, ROWS, LANES), BF16),
            pltpu.VMEM((ROWS, 4 * EIG), BF16),
            pltpu.VMEM((BANDS, PAIRS, 4 * EIG), F32),
            pltpu.VMEM((BANDS, 8, 8, 4 * EIG), F32),
            pltpu.VMEM((BANDS, 8, 4 * EIG), F32),
            pltpu.VMEM((8, 8, 2 * EIG), F32),
            pltpu.VMEM((2, 8, 8, EIG), F32),
            dma((2,)),
            dma((STRIPS + 1,)),
            dma((SETS,)),
            dma((6,)),
            dma((2, 2)),
            dma((2, 2)),
            dma((SETS, 3)),
            dma((SETS, 3)),
            dma((1,)),
            dma((BANDS,)),
            dma((2,)),
            dma((2,)),
        ],
        compiler_params=pltpu.CompilerParams(
            collective_id=0, has_side_effects=True, vmem_limit_bytes=VMEM_LIMIT
        ),
        name="projections",
    )(g_cell, pocc, pemp, occ, emp, jnp.asarray(t1), jnp.asarray(t2), eigvecs)


def shards(occupied, empty, pair_occ, pair_emp, g_cell, eigvecs):
    occ = jnp.transpose(occupied, (1, 2, 3, 0)).reshape(2, N * N, LANES)
    emp = jnp.transpose(empty, (1, 2, 3, 0)).reshape(2, N * N, LANES)
    return run(g_cell, pair_occ.reshape(1, PAIRS), pair_emp.reshape(1, PAIRS), occ, emp, eigvecs)


def solution(mesh):
    in_specs = (
        P(None, "grid", None, None),
        P(None, "grid", None, None),
        P("band"),
        P("band"),
        P("grid"),
        P(None, "grid", "band"),
    )
    out_specs = P(None, "grid", "band")
    return jax.shard_map(shards, mesh=mesh, in_specs=in_specs, out_specs=out_specs, check_vma=False)
```
